32 devices in a mesh: clip: 8 (over y, x, core), sp: 4 (over z).
Axes of the slice: x: 2, y: 2, z: 4, core: 2. Of those that a mesh axis runs over, the one named last changes fastest.
Arguments:
- queries: bfloat16 [4096, 6144], P(('clip', 'sp')), parts along dimension 0, may hold values from -256 to 256
- key_codes: bfloat16 [4096, 1024], P(('clip', 'sp')), parts along dimension 0, may hold values from -7 to 7
- value_codes: bfloat16 [4096, 1024], P(('clip', 'sp')), parts along dimension 0, may hold values from -6 to 6
- key_scales: bfloat16 [32, 8], P(('clip', 'sp')), parts along dimension 0, may hold values from 0.25 to 2
- value_scales: bfloat16 [32, 8], P(('clip', 'sp')), parts along dimension 0, may hold values from 0.25 to 2
- masks: int32 [384, 4, 4], P('clip'), parts along dimension 0, may hold values from 0 to 1, as said below
Outputs:
- attended: bfloat16 [4096, 6144], P(('clip', 'sp')), parts along dimension 0
The draws below stay inside these ranges and needn't reach their ends.
There are 8 independent parts, one for each index of `clip`. The reference program is written for one: setup_inputs(seed, part) draws one part's arguments, and reference() takes and returns one part's arrays. A program takes and returns all parts, laid end to end along the dimension named above; each array names one. Nothing has to cross between parts.
Inputs may be any that keep to these rules, and one draw needn't show every extreme that they name: masks[h, a, b] is 1 where query tile a of head h attends to key tile b and 0 where it does not; every diagonal tile (a == b) is 1; the share of kept tiles differs from head to head.
All inputs are finite; a program needn't handle non-finite values.
Results may differ from the reference program's by a relative error of at most 0.0038.
Values may be sent and summed in bfloat16 or wider, within the bound.
A program may use at most 128 MiB of HBM per device.

```python
import math
import jax
import jax.numpy as jnp
from jax import lax

QH = 48
KVH = 8
HD = 128
TILE = 128
SEQ = 512
TILES = 4


def pair_draw(key):
    base = jax.random.fold_in(key, 11)
    draw_keys = jax.random.split(base, 2)
    key_part = jnp.clip(jax.random.normal(draw_keys[0], (SEQ, KVH, HD), jnp.float32), -6.0, 6.0)
    query_part = jnp.clip(jax.random.normal(draw_keys[1], (SEQ, QH, HD), jnp.float32), -6.0, 6.0)
    return (query_part, key_part)


def draw_queries(key, part):
    query_part, key_part = pair_draw(key)
    return query_part.reshape(SEQ, QH * HD).astype(jnp.bfloat16)


def draw_key_codes(key, part):
    query_part, key_part = pair_draw(key)
    return key_part.reshape(SEQ, KVH * HD).astype(jnp.bfloat16)


def draw_masks(key, part):
    base = jax.random.fold_in(key, 23)
    draw_keys = jax.random.split(base, 2)
    density = jax.random.randint(draw_keys[0], (QH, 1, 1), 1, TILES + 1)
    rolls = jax.random.randint(draw_keys[1], (QH, TILES, TILES), 0, TILES)
    diagonal = jnp.eye(TILES, dtype=jnp.int32) > 0
    return jnp.where((rolls < density) | diagonal[None], 1, 0).astype(jnp.int32)


def steps_of(stream_key, extent, cuts, least, largest):
    factor_of, own = 1.0, jax.random.fold_in(stream_key, 6)
    for dim, shards_of in cuts:
        steps = jnp.exp(jax.random.uniform(jax.random.fold_in(own, dim), (shards_of,), jnp.float32, least / len(cuts), largest / len(cuts)))
        factor_of = factor_of * jnp.repeat(steps, extent[dim] // shards_of).reshape([-1 if axis == dim else 1 for axis in range(len(extent))])
    return factor_of


def noise(key, dims, width, bound, cuts=(), kind=jnp.bfloat16):
    level = steps_of(key, dims, cuts, -0.22, 0.18) if cuts else 1.0
    entries = jax.random.normal(key, dims, jnp.float32) * width * level
    return jnp.minimum(jnp.maximum(entries, -bound), bound).astype(kind)


def setup_inputs(seed: int = 0, part: int = 0) -> dict:
    streams_of = jax.random.split(jax.random.key(seed), 7)
    part_keys = jax.random.split(jax.random.fold_in(streams_of[6], part), 7)
    return {
        "queries": draw_queries(jax.random.fold_in(jax.random.fold_in(streams_of[6], part), 71), part),
        "key_codes": draw_key_codes(jax.random.fold_in(jax.random.fold_in(streams_of[6], part), 71), part),
        "value_codes": noise(part_keys[2], (SEQ, KVH * HD), 1.0, 6.0, ((0, 4),)),
        "key_scales": jnp.clip(jnp.exp(math.log(2.0) - 2.0794415 * jax.random.uniform(part_keys[3], (TILES, KVH), jnp.float32) ** steps_of(part_keys[3], (TILES, KVH), ((0, 4),), -0.2, 0.2)), 0.25, 2.0).astype(jnp.bfloat16),
        "value_scales": jnp.clip(jnp.exp(math.log(2.0) - 2.0794415 * jax.random.uniform(part_keys[4], (TILES, KVH), jnp.float32) ** steps_of(part_keys[4], (TILES, KVH), ((0, 4),), -0.2, 0.2)), 0.25, 2.0).astype(jnp.bfloat16),
        "masks": draw_masks(jax.random.fold_in(jax.random.fold_in(streams_of[6], part), 71), part),
    }


def reference(queries, key_codes, value_codes, key_scales, value_scales, masks):
    per_group = QH // KVH
    query_heads = queries.reshape(SEQ, QH, HD)
    key_heads = key_codes.reshape(SEQ, KVH, HD)
    value_heads = value_codes.reshape(SEQ, KVH, HD)
    key_tokens = jnp.repeat(key_scales.astype(jnp.float32), TILE, axis=0)
    value_tokens = jnp.repeat(value_scales.astype(jnp.float32), TILE, axis=0)
    inverse = 1.0 / math.sqrt(HD)

    def one_head(head_index):
        shared = head_index // per_group
        query_one = lax.dynamic_index_in_dim(query_heads, head_index, 1, keepdims=False).astype(jnp.float32)
        key_one = lax.dynamic_index_in_dim(key_heads, shared, 1, keepdims=False).astype(jnp.float32)
        value_one = lax.dynamic_index_in_dim(value_heads, shared, 1, keepdims=False)
        key_scale = lax.dynamic_index_in_dim(key_tokens, shared, 1, keepdims=False)
        value_scale = lax.dynamic_index_in_dim(value_tokens, shared, 1, keepdims=False)
        scores = jnp.dot(query_one, key_one.T, preferred_element_type=jnp.float32)
        scores = scores * key_scale[None, :] * inverse
        tile_mask = lax.dynamic_index_in_dim(masks, head_index, 0, keepdims=False)
        keep = jnp.repeat(jnp.repeat(tile_mask, TILE, axis=0), TILE, axis=1) > 0
        scores = jnp.where(keep, scores, -1e+30)
        highest = lax.optimization_barrier(jnp.max(scores, axis=1, keepdims=True))
        expo = jnp.where(keep, jnp.exp(scores - highest), 0.0)
        total = lax.optimization_barrier(jnp.sum(expo, axis=1))
        weights = (expo * value_scale[None, :]).astype(jnp.bfloat16)
        summed = jnp.dot(weights, value_one, preferred_element_type=jnp.float32)
        return (summed / total[:, None]).astype(jnp.bfloat16)
    result = lax.map(one_head, jnp.arange(QH, dtype=jnp.int32))
    return jnp.transpose(result, (1, 0, 2)).reshape(SEQ, QH * HD)
```

```python
import functools
import math

import jax
import jax.numpy as jnp
from jax import lax
from jax.experimental import pallas as pl
from jax.experimental.pallas import tpu as pltpu
from jax.sharding import PartitionSpec as P

NEGATIVE = -1e30
MESH = pl.DeviceIdType.MESH


def attention_kernel(
    devices, kv_heads, per_group, head, rows,
    q_hbm, k_hbm, v_hbm, key_scale_ref, value_scale_ref, masks_ref, out_hbm,
    q_ref, codes, scales, tops, totals, sums, stage,
    q_sem, own_sem, send_right, send_left, scale_right, scale_left,
    recv_sem, scale_recv, out_sem,
):
    me = lax.axis_index("sp")
    has_left = me > 0
    has_right = me < devices - 1
    last_step = jnp.maximum(me, devices - 1 - me)
    wide = per_group * head
    factor = math.log2(math.e) / math.sqrt(head)

    def own_copies(g):
        columns = pl.ds(pl.multiple_of(g * head, head), head)
        return (
            pltpu.make_async_copy(
                k_hbm.at[:, columns], codes.at[me, g, pl.ds(0, rows)], own_sem.at[g, 0]
            ),
            pltpu.make_async_copy(
                v_hbm.at[:, columns], codes.at[me, g, pl.ds(rows, rows)], own_sem.at[g, 1]
            ),
        )

    def q_copy():
        return pltpu.make_async_copy(q_hbm, q_ref, q_sem)

    def code_copy(tile, g, to, send):
        return pltpu.make_async_remote_copy(
            src_ref=codes.at[tile, g],
            dst_ref=codes.at[tile, g],
            send_sem=send.at[tile],
            recv_sem=recv_sem.at[tile, g],
            device_id={"sp": to},
            device_id_type=MESH,
        )

    def scale_copy(tile, to, send):
        return pltpu.make_async_remote_copy(
            src_ref=scales.at[tile],
            dst_ref=scales.at[tile],
            send_sem=send.at[tile],
            recv_sem=scale_recv.at[tile],
            device_id={"sp": to},
            device_id_type=MESH,
        )

    def out_copy(g):
        columns = pl.ds(pl.multiple_of(g * wide, wide), wide)
        return pltpu.make_async_copy(stage.at[:, columns], out_hbm.at[:, columns], out_sem.at[g])

    for g in range(kv_heads):
        for copy in own_copies(g):
            copy.start()
    q_copy().start()

    barrier = pltpu.get_barrier_semaphore()

    @pl.when(has_left)
    def _():
        pl.semaphore_signal(barrier, inc=1, device_id={"sp": me - 1}, device_id_type=MESH)

    @pl.when(has_right)
    def _():
        pl.semaphore_signal(barrier, inc=1, device_id={"sp": me + 1}, device_id_type=MESH)

    def column(ref):
        spread = jnp.broadcast_to(ref[...].astype(jnp.float32), (kv_heads, kv_heads))
        place = lax.broadcasted_iota(jnp.int32, (kv_heads, kv_heads), 0)
        other = lax.broadcasted_iota(jnp.int32, (kv_heads, kv_heads), 1)
        picked = jnp.sum(jnp.where(place == other, spread, 0.0), axis=1, keepdims=True)
        return jnp.broadcast_to(picked, (kv_heads, head))

    scales[me] = jnp.concatenate(
        [column(key_scale_ref), column(value_scale_ref)], axis=0
    ).astype(jnp.bfloat16)

    pl.semaphore_wait(barrier, has_left.astype(jnp.int32) + has_right.astype(jnp.int32))

    @pl.when(has_right)
    def _():
        scale_copy(me, me + 1, scale_right).start()

    @pl.when(has_left)
    def _():
        scale_copy(me, me - 1, scale_left).start()

    def send_own(g, carry):
        for copy in own_copies(g):
            copy.wait()

        @pl.when(has_right)
        def _():
            code_copy(me, g, me + 1, send_right).start()

        @pl.when(has_left)
        def _():
            code_copy(me, g, me - 1, send_left).start()

        return carry

    lax.fori_loop(0, kv_heads, send_own, 0)
    q_copy().wait()

    ones = jnp.ones((rows, head), jnp.bfloat16)

    def attend(tile, g, first):
        both = scales[tile].astype(jnp.float32)
        place = lax.broadcasted_iota(jnp.int32, both.shape, 0)
        key_scale = jnp.sum(jnp.where(place == g, both, 0.0), axis=0, keepdims=True)
        value_scale = jnp.sum(jnp.where(place == g + kv_heads, both, 0.0), axis=0, keepdims=True)
        key_scale = key_scale * factor
        queries = jnp.concatenate(
            [
                q_ref[:, pl.ds(pl.multiple_of((g * per_group + r) * head, head), head)]
                for r in range(per_group)
            ],
            axis=0,
        )
        keys = codes[tile, g, :rows, :]
        values = jnp.concatenate([codes[tile, g, rows:, :], ones], axis=1)
        raw = lax.dot_general(
            queries, keys, (((1,), (1,)), ((), ())), preferred_element_type=jnp.float32
        )
        expo, rescale = [], []
        for r in range(per_group):
            part = pl.ds(r * rows, rows)
            keep = masks_ref[g * per_group + r, me, tile]
            bias = jnp.where(keep > 0, 0.0, NEGATIVE).astype(jnp.float32)
            scores = raw[r * rows : (r + 1) * rows] * key_scale + bias
            top = jnp.broadcast_to(jnp.max(scores, axis=1, keepdims=True), (rows, head))
            if not first:
                before = tops[g, part, :]
                top = jnp.maximum(before, top)
                rescale.append(jnp.exp2(before - top))
            tops[g, part, :] = top
            expo.append(jnp.exp2(scores - top).astype(jnp.bfloat16))
        added = jnp.dot(
            jnp.concatenate(expo, axis=0), values, preferred_element_type=jnp.float32
        )
        for r in range(per_group):
            part = pl.ds(r * rows, rows)
            piece = added[r * rows : (r + 1) * rows]
            if first:
                sums[g, part, :] = piece[:, :head] * value_scale
                totals[g, part, :] = piece[:, head:]
            else:
                sums[g, part, :] = sums[g, part, :] * rescale[r] + piece[:, :head] * value_scale
                totals[g, part, :] = totals[g, part, :] * rescale[r] + piece[:, head:]

    def attend_own(g, carry):
        attend(me, g, True)
        return carry

    lax.fori_loop(0, kv_heads, attend_own, 0)

    def step_body(step, carry):
        left, right = me - step, me + step
        from_left, from_right = left >= 0, right <= devices - 1

        @pl.when(from_left)
        def _():
            scale_copy(left, me, scale_right).wait_recv()

            @pl.when(has_right)
            def _():
                scale_copy(left, me + 1, scale_right).start()

        @pl.when(from_right)
        def _():
            scale_copy(right, me, scale_left).wait_recv()

            @pl.when(has_left)
            def _():
                scale_copy(right, me - 1, scale_left).start()

        def chunk_body(g, inner):
            @pl.when(from_left)
            def _():
                code_copy(left, g, me, send_right).wait_recv()

                @pl.when(has_right)
                def _():
                    code_copy(left, g, me + 1, send_right).start()

            @pl.when(from_right)
            def _():
                code_copy(right, g, me, send_left).wait_recv()

                @pl.when(has_left)
                def _():
                    code_copy(right, g, me - 1, send_left).start()

            @pl.when(from_left)
            def _():
                attend(left, g, False)

            @pl.when(from_right)
            def _():
                attend(right, g, False)

            @pl.when(step == last_step)
            def _():
                for r in range(per_group):
                    part = pl.ds(r * rows, rows)
                    place = pl.ds(pl.multiple_of((g * per_group + r) * head, head), head)
                    stage[:, place] = (sums[g, part, :] / totals[g, part, :]).astype(jnp.bfloat16)
                out_copy(g).start()

            return inner

        lax.fori_loop(0, kv_heads, chunk_body, 0)
        return carry

    lax.fori_loop(1, last_step + 1, step_body, 0)

    def drain(tile, carry):
        @pl.when(jnp.logical_and(tile <= me, has_right))
        def _():
            scale_copy(tile, me + 1, scale_right).wait_send()
            pltpu.make_async_copy(codes.at[tile], codes.at[tile], send_right.at[tile]).wait()

        @pl.when(jnp.logical_and(tile >= me, has_left))
        def _():
            scale_copy(tile, me - 1, scale_left).wait_send()
            pltpu.make_async_copy(codes.at[tile], codes.at[tile], send_left.at[tile]).wait()

        return carry

    lax.fori_loop(0, devices, drain, 0)

    def flush(g, carry):
        out_copy(g).wait()
        return carry

    lax.fori_loop(0, kv_heads, flush, 0)


def local(devices, queries, key_codes, value_codes, key_scales, value_scales, masks):
    rows, width = queries.shape
    kv_heads = key_scales.shape[1]
    heads = masks.shape[0]
    head = width // heads
    per_group = heads // kv_heads
    tall = per_group * rows
    hbm = pl.BlockSpec(memory_space=pltpu.HBM)
    vmem = pl.BlockSpec(memory_space=pltpu.VMEM)
    smem = pl.BlockSpec(memory_space=pltpu.SMEM)
    dma = pltpu.SemaphoreType.DMA
    scores = heads * rows * rows * devices
    return pl.pallas_call(
        functools.partial(attention_kernel, devices, kv_heads, per_group, head, rows),
        out_shape=jax.ShapeDtypeStruct((rows, width), jnp.bfloat16),
        in_specs=[hbm, hbm, hbm, vmem, vmem, smem],
        out_specs=hbm,
        scratch_shapes=[
            pltpu.VMEM((rows, width), jnp.bfloat16),
            pltpu.VMEM((devices, kv_heads, 2 * rows, head), jnp.bfloat16),
            pltpu.VMEM((devices, 2 * kv_heads, head), jnp.bfloat16),
            pltpu.VMEM((kv_heads, tall, head), jnp.float32),
            pltpu.VMEM((kv_heads, tall, head), jnp.float32),
            pltpu.VMEM((kv_heads, tall, head), jnp.float32),
            pltpu.VMEM((rows, width), jnp.bfloat16),
            dma,
            dma((kv_heads, 2)),
            dma((devices,)),
            dma((devices,)),
            dma((devices,)),
            dma((devices,)),
            dma((devices, kv_heads)),
            dma((devices,)),
            dma((kv_heads,)),
        ],
        compiler_params=pltpu.CompilerParams(
            collective_id=0, has_side_effects=True, vmem_limit_bytes=48 * 1024 * 1024
        ),
        cost_estimate=pl.CostEstimate(
            flops=4 * scores * head, bytes_accessed=4 * rows * width, transcendentals=scores
        ),
    )(queries, key_codes, value_codes, key_scales, value_scales, masks)


def solution(mesh):
    both = P(("clip", "sp"), None)
    return jax.shard_map(
        functools.partial(local, mesh.shape["sp"]),
        mesh=mesh,
        in_specs=(both, both, both, both, both, P("clip", None, None)),
        out_specs=both,
        check_vma=False,
    )
```

```python
import functools
import math

import jax
import jax.numpy as jnp
from jax import lax
from jax.experimental import pallas as pl
from jax.experimental.pallas import tpu as pltpu
from jax.sharding import PartitionSpec as P

NEGATIVE = -1e30
MESH = pl.DeviceIdType.MESH


def attention_kernel(
    devices, kv_heads, per_group, head, rows,
    q_hbm, k_hbm, v_hbm, key_scale_hbm, value_scale_hbm, masks_hbm, out_hbm,
    q_ref, codes, scales, tops, totals, sums, stage, key_scale_ref, value_scale_ref, masks_ref,
    q_sem, small_sem, own_sem, send_right, send_left, scale_right, scale_left,
    recv_sem, scale_recv, out_sem,
):
    me = lax.axis_index("sp")
    to_right = lax.rem(me + 1, devices)
    to_left = lax.rem(me + devices - 1, devices)
    full = (devices - 1) // 2
    split = devices % 2 == 0
    half = kv_heads // 2
    wide = per_group * head
    factor = math.log2(math.e) / math.sqrt(head)

    barrier = pltpu.get_barrier_semaphore()
    for neighbour in (to_left, to_right):
        pl.semaphore_signal(barrier, inc=1, device_id={"sp": neighbour}, device_id_type=MESH)

    def own_copies(g):
        columns = pl.ds(pl.multiple_of(g * head, head), head)
        return (
            pltpu.make_async_copy(
                k_hbm.at[:, columns], codes.at[me, g, pl.ds(0, rows)], own_sem.at[g, 0]
            ),
            pltpu.make_async_copy(
                v_hbm.at[:, columns], codes.at[me, g, pl.ds(rows, rows)], own_sem.at[g, 1]
            ),
        )

    def q_copy():
        return pltpu.make_async_copy(q_hbm, q_ref, q_sem)

    def small_copies():
        return (
            pltpu.make_async_copy(key_scale_hbm, key_scale_ref, small_sem.at[0]),
            pltpu.make_async_copy(value_scale_hbm, value_scale_ref, small_sem.at[1]),
            pltpu.make_async_copy(masks_hbm, masks_ref, small_sem.at[2]),
        )

    def code_copy(tile, g, to, send):
        return pltpu.make_async_remote_copy(
            src_ref=codes.at[tile, g],
            dst_ref=codes.at[tile, g],
            send_sem=send.at[tile],
            recv_sem=recv_sem.at[tile, g],
            device_id={"sp": to},
            device_id_type=MESH,
        )

    def scale_copy(tile, to, send):
        return pltpu.make_async_remote_copy(
            src_ref=scales.at[tile],
            dst_ref=scales.at[tile],
            send_sem=send.at[tile],
            recv_sem=scale_recv.at[tile],
            device_id={"sp": to},
            device_id_type=MESH,
        )

    def out_copy(g):
        columns = pl.ds(pl.multiple_of(g * wide, wide), wide)
        return pltpu.make_async_copy(stage.at[:, columns], out_hbm.at[:, columns], out_sem.at[g])

    for copy in small_copies():
        copy.start()
    for g in range(kv_heads):
        for copy in own_copies(g):
            copy.start()
    q_copy().start()

    def column(ref):
        spread = jnp.broadcast_to(ref[...].astype(jnp.float32), (kv_heads, kv_heads))
        place = lax.broadcasted_iota(jnp.int32, (kv_heads, kv_heads), 0)
        other = lax.broadcasted_iota(jnp.int32, (kv_heads, kv_heads), 1)
        picked = jnp.sum(jnp.where(place == other, spread, 0.0), axis=1, keepdims=True)
        return jnp.broadcast_to(picked, (kv_heads, head))

    for copy in small_copies():
        copy.wait()
    scales[me] = jnp.concatenate(
        [column(key_scale_ref), column(value_scale_ref)], axis=0
    ).astype(jnp.bfloat16)

    pl.semaphore_wait(barrier, 2)

    def send_scales(tile, hop, rightward):
        if rightward:
            @pl.when(hop < (full + 1 if split else full))
            def _():
                scale_copy(tile, to_right, scale_right).start()
        else:
            @pl.when(hop < full)
            def _():
                scale_copy(tile, to_left, scale_left).start()

    def send_codes(tile, g, hop, rightward):
        go = hop < full
        if split:
            mine = g < half if rightward else g >= half
            go = jnp.logical_or(go, jnp.logical_and(hop == full, mine))

        @pl.when(go)
        def _():
            if rightward:
                code_copy(tile, g, to_right, send_right).start()
            else:
                code_copy(tile, g, to_left, send_left).start()

    send_scales(me, 0, True)
    send_scales(me, 0, False)

    def send_own(g, carry):
        for copy in own_copies(g):
            copy.wait()
        send_codes(me, g, 0, True)
        send_codes(me, g, 0, False)
        return carry

    lax.fori_loop(0, kv_heads, send_own, 0)
    q_copy().wait()

    ones = jnp.ones((rows, head), jnp.bfloat16)

    def attend(tile, g, first=False, last=False):
        both = scales[tile].astype(jnp.float32)
        place = lax.broadcasted_iota(jnp.int32, both.shape, 0)
        key_scale = jnp.sum(jnp.where(place == g, both, 0.0), axis=0, keepdims=True)
        value_scale = jnp.sum(jnp.where(place == g + kv_heads, both, 0.0), axis=0, keepdims=True)
        key_scale = key_scale * factor
        queries = jnp.concatenate(
            [
                q_ref[:, pl.ds(pl.multiple_of((g * per_group + r) * head, head), head)]
                for r in range(per_group)
            ],
            axis=0,
        )
        keys = codes[tile, g, :rows, :]
        values = jnp.concatenate([codes[tile, g, rows:, :], ones], axis=1)
        raw = lax.dot_general(
            queries, keys, (((1,), (1,)), ((), ())), preferred_element_type=jnp.float32
        )
        expo, rescale = [], []
        for r in range(per_group):
            part = pl.ds(r * rows, rows)
            keep = masks_ref[me, tile, g * per_group + r]
            bias = jnp.where(keep > 0, 0.0, NEGATIVE).astype(jnp.float32)
            scores = raw[r * rows : (r + 1) * rows] * key_scale + bias
            top = jnp.broadcast_to(jnp.max(scores, axis=1, keepdims=True), (rows, head))
            if not first:
                before = tops[g, part, :]
                top = jnp.maximum(before, top)
                rescale.append(jnp.exp2(before - top))
            if not last:
                tops[g, part, :] = top
            expo.append(jnp.exp2(scores - top).astype(jnp.bfloat16))
        added = jnp.dot(
            jnp.concatenate(expo, axis=0), values, preferred_element_type=jnp.float32
        )
        for r in range(per_group):
            part = pl.ds(r * rows, rows)
            piece = added[r * rows : (r + 1) * rows]
            product = piece[:, :head] * value_scale
            total = piece[:, head:]
            if not first:
                product = product + sums[g, part, :] * rescale[r]
                total = total + totals[g, part, :] * rescale[r]
            if last:
                place = pl.ds(pl.multiple_of((g * per_group + r) * head, head), head)
                stage[:, place] = (product / total).astype(jnp.bfloat16)
            else:
                sums[g, part, :] = product
                totals[g, part, :] = total
        if last:
            out_copy(g).start()

    def attend_own(g, carry):
        attend(me, g, first=True)
        return carry

    lax.fori_loop(0, kv_heads, attend_own, 0)

    def step_body(step, carry):
        left = lax.rem(me - step + devices, devices)
        right = lax.rem(me + step, devices)
        scale_copy(left, to_right, scale_right).wait_recv()
        send_scales(left, step, True)
        scale_copy(right, to_left, scale_left).wait_recv()
        send_scales(right, step, False)

        def chunk_body(g, inner):
            code_copy(left, g, to_right, send_right).wait_recv()
            send_codes(left, g, step, True)
            code_copy(right, g, to_left, send_left).wait_recv()
            send_codes(right, g, step, False)
            attend(left, g)
            attend(right, g)
            return inner

        lax.fori_loop(0, kv_heads, chunk_body, 0)
        return carry

    lax.fori_loop(1, full + 1, step_body, 0)

    if split:
        across = lax.rem(me + devices // 2, devices)
        scale_copy(across, to_right, scale_right).wait_recv()

        def across_body(g, carry):
            code_copy(across, g, to_right, send_right).wait_recv()
            attend(across, g, last=True)
            code_copy(across, g + half, to_left, send_left).wait_recv()
            attend(across, g + half, last=True)
            return carry

        lax.fori_loop(0, half, across_body, 0)
    else:

        def finish(g, carry):
            for r in range(per_group):
                part = pl.ds(r * rows, rows)
                place = pl.ds(pl.multiple_of((g * per_group + r) * head, head), head)
                stage[:, place] = (sums[g, part, :] / totals[g, part, :]).astype(jnp.bfloat16)
            out_copy(g).start()
            return carry

        lax.fori_loop(0, kv_heads, finish, 0)

    def drain(hop, carry):
        left = lax.rem(me - hop + devices, devices)
        right = lax.rem(me + hop, devices)
        scale_copy(left, to_right, scale_right).wait_send()
        scale_copy(right, to_left, scale_left).wait_send()
        pltpu.make_async_copy(codes.at[left], codes.at[left], send_right.at[left]).wait()
        pltpu.make_async_copy(codes.at[right], codes.at[right], send_left.at[right]).wait()
        return carry

    lax.fori_loop(0, full, drain, 0)
    if split:
        left = lax.rem(me - full + devices, devices)
        right = lax.rem(me + full, devices)
        first, second = pl.ds(0, half), pl.ds(half, half)
        scale_copy(left, to_right, scale_right).wait_send()
        pltpu.make_async_copy(
            codes.at[left, first], codes.at[left, first], send_right.at[left]
        ).wait()
        pltpu.make_async_copy(
            codes.at[right, second], codes.at[right, second], send_left.at[right]
        ).wait()

    def flush(g, carry):
        out_copy(g).wait()
        return carry

    lax.fori_loop(0, kv_heads, flush, 0)


def local(devices, queries, key_codes, value_codes, key_scales, value_scales, masks):
    rows, width = queries.shape
    kv_heads = key_scales.shape[1]
    masks = jnp.transpose(masks, (1, 2, 0))
    heads = masks.shape[2]
    head = width // heads
    per_group = heads // kv_heads
    tall = per_group * rows
    hbm = pl.BlockSpec(memory_space=pltpu.HBM)
    dma = pltpu.SemaphoreType.DMA
    scores = heads * rows * rows * devices
    return pl.pallas_call(
        functools.partial(attention_kernel, devices, kv_heads, per_group, head, rows),
        out_shape=jax.ShapeDtypeStruct((rows, width), jnp.bfloat16),
        in_specs=[hbm] * 6,
        out_specs=hbm,
        scratch_shapes=[
            pltpu.VMEM((rows, width), jnp.bfloat16),
            pltpu.VMEM((devices, kv_heads, 2 * rows, head), jnp.bfloat16),
            pltpu.VMEM((devices, 2 * kv_heads, head), jnp.bfloat16),
            pltpu.VMEM((kv_heads, tall, head), jnp.float32),
            pltpu.VMEM((kv_heads, tall, head), jnp.float32),
            pltpu.VMEM((kv_heads, tall, head), jnp.float32),
            pltpu.VMEM((rows, width), jnp.bfloat16),
            pltpu.VMEM(key_scales.shape, jnp.bfloat16),
            pltpu.VMEM(value_scales.shape, jnp.bfloat16),
            pltpu.SMEM(masks.shape, jnp.int32),
            dma,
            dma((3,)),
            dma((kv_heads, 2)),
            dma((devices,)),
            dma((devices,)),
            dma((devices,)),
            dma((devices,)),
            dma((devices, kv_heads)),
            dma((devices,)),
            dma((kv_heads,)),
        ],
        compiler_params=pltpu.CompilerParams(
            collective_id=0, has_side_effects=True, vmem_limit_bytes=63 * 1024 * 1024
        ),
        cost_estimate=pl.CostEstimate(
            flops=4 * scores * head, bytes_accessed=4 * rows * width, transcendentals=scores
        ),
    )(queries, key_codes, value_codes, key_scales, value_scales, masks)


def solution(mesh):
    both = P(("clip", "sp"), None)
    return jax.shard_map(
        functools.partial(local, mesh.shape["sp"]),
        mesh=mesh,
        in_specs=(both, both, both, both, both, P("clip", None, None)),
        out_specs=both,
        check_vma=False,
    )
```

```python
import functools
import math

import jax
import jax.numpy as jnp
from jax import lax
from jax.experimental import pallas as pl
from jax.experimental.pallas import tpu as pltpu
from jax.sharding import PartitionSpec as P

NEGATIVE = -1e30
MESH = pl.DeviceIdType.MESH


def attention_kernel(
    devices, kv_heads, per_group, head, rows,
    q_hbm, k_hbm, v_hbm, key_scale_hbm, value_scale_hbm, masks_hbm, out_hbm,
    q_ref, q_turned, codes, scales, tops, totals, sums, stage,
    key_scale_ref, value_scale_ref, masks_ref,
    q_sem, small_sem, own_sem, send_right, send_left, scale_right, scale_left,
    recv_sem, scale_recv, out_sem,
):
    me = lax.axis_index("sp")
    has_left = me > 0
    has_right = me < devices - 1
    middle = jnp.logical_and(has_left, has_right)
    last_step = jnp.maximum(me, devices - 1 - me)
    wide = per_group * head
    pair = 2 if per_group % 2 == 0 else 1
    factor = math.log2(math.e) / math.sqrt(head)

    barrier = pltpu.get_barrier_semaphore()

    @pl.when(has_left)
    def _():
        pl.semaphore_signal(barrier, inc=1, device_id={"sp": me - 1}, device_id_type=MESH)

    @pl.when(has_right)
    def _():
        pl.semaphore_signal(barrier, inc=1, device_id={"sp": me + 1}, device_id_type=MESH)

    def own_copies(g):
        columns = pl.ds(pl.multiple_of(g * head, head), head)
        return (
            pltpu.make_async_copy(
                k_hbm.at[:, columns], codes.at[me, g, pl.ds(0, rows)], own_sem.at[g, 0]
            ),
            pltpu.make_async_copy(
                v_hbm.at[:, columns], codes.at[me, g, pl.ds(rows, rows)], own_sem.at[g, 1]
            ),
        )

    def q_copy():
        return pltpu.make_async_copy(q_hbm, q_ref, q_sem)

    def small_copies():
        return (
            pltpu.make_async_copy(key_scale_hbm, key_scale_ref, small_sem.at[0]),
            pltpu.make_async_copy(value_scale_hbm, value_scale_ref, small_sem.at[1]),
            pltpu.make_async_copy(masks_hbm, masks_ref, small_sem.at[2]),
        )

    def code_copy(tile, g, to, send):
        return pltpu.make_async_remote_copy(
            src_ref=codes.at[tile, g],
            dst_ref=codes.at[tile, g],
            send_sem=send.at[tile],
            recv_sem=recv_sem.at[tile, g],
            device_id={"sp": to},
            device_id_type=MESH,
        )

    def scale_copy(tile, to, send):
        return pltpu.make_async_remote_copy(
            src_ref=scales.at[tile],
            dst_ref=scales.at[tile],
            send_sem=send.at[tile],
            recv_sem=scale_recv.at[tile],
            device_id={"sp": to},
            device_id_type=MESH,
        )

    def out_copy(g):
        columns = pl.ds(pl.multiple_of(g * wide, wide), wide)
        return pltpu.make_async_copy(stage.at[:, columns], out_hbm.at[:, columns], out_sem.at[g])

    for copy in small_copies():
        copy.start()
    for g in range(kv_heads):
        for copy in own_copies(g):
            copy.start()
    q_copy().start()

    def column(ref):
        spread = jnp.broadcast_to(ref[...].astype(jnp.float32), (kv_heads, kv_heads))
        place = lax.broadcasted_iota(jnp.int32, (kv_heads, kv_heads), 0)
        other = lax.broadcasted_iota(jnp.int32, (kv_heads, kv_heads), 1)
        picked = jnp.sum(jnp.where(place == other, spread, 0.0), axis=1, keepdims=True)
        return jnp.broadcast_to(picked, (kv_heads, head))

    for copy in small_copies():
        copy.wait()
    scales[me] = jnp.concatenate(
        [column(key_scale_ref), column(value_scale_ref)], axis=0
    ).astype(jnp.bfloat16)

    pl.semaphore_wait(barrier, has_left.astype(jnp.int32) + has_right.astype(jnp.int32))

    @pl.when(has_right)
    def _():
        scale_copy(me, me + 1, scale_right).start()

    @pl.when(has_left)
    def _():
        scale_copy(me, me - 1, scale_left).start()

    def send_own(g, carry):
        for copy in own_copies(g):
            copy.wait()

        @pl.when(has_right)
        def _():
            code_copy(me, g, me + 1, send_right).start()

        @pl.when(has_left)
        def _():
            code_copy(me, g, me - 1, send_left).start()

        return carry

    lax.fori_loop(0, kv_heads, send_own, 0)
    q_copy().wait()

    ones = jnp.ones((16, rows), jnp.bfloat16)

    def attend(tile, g, first=False):
        both = scales[tile].astype(jnp.float32)
        place = lax.broadcasted_iota(jnp.int32, both.shape, 0)
        key_scale = jnp.sum(jnp.where(place == g, both, 0.0), axis=0, keepdims=True)
        value_scale = jnp.sum(jnp.where(place == g + kv_heads, both, 0.0), axis=0, keepdims=True)
        key_scale = jnp.concatenate([key_scale * factor] * pair, axis=1)
        value_scale = jnp.concatenate([value_scale] * pair, axis=1)
        keys = codes[tile, g, :rows, :]
        values = jnp.concatenate([jnp.transpose(codes[tile, g, rows:, :]), ones], axis=0)
        for r in range(0, per_group, pair):
            columns = pl.ds(r * rows, pair * rows)
            if first:
                queries = jnp.concatenate(
                    [
                        jnp.transpose(
                            q_ref[:, pl.ds(pl.multiple_of((g * per_group + o) * head, head), head)]
                        )
                        for o in range(r, r + pair)
                    ],
                    axis=1,
                )
                q_turned[g, :, columns] = queries
            else:
                queries = q_turned[g, :, columns]
            raw = jnp.dot(keys, queries, preferred_element_type=jnp.float32)
            bias = jnp.concatenate(
                [
                    jnp.full(
                        (1, rows),
                        jnp.where(masks_ref[me, tile, g * per_group + o] > 0, 0.0, NEGATIVE),
                        jnp.float32,
                    )
                    for o in range(r, r + pair)
                ],
                axis=1,
            )
            top = jnp.max(raw, axis=0, keepdims=True) * key_scale + bias
            if not first:
                before = tops[g, :, columns]
                top = jnp.maximum(before, top)
                rescale = jnp.exp2(before - top)
            tops[g, :, columns] = top
            expo = jnp.exp2(raw * key_scale - (top - bias)).astype(jnp.bfloat16)
            added = jnp.dot(values, expo, preferred_element_type=jnp.float32)
            product = added[:head] * value_scale
            total = added[head : head + 1]
            if not first:
                product = product + sums[g, :, columns] * rescale
                total = total + totals[g, :, columns] * rescale
            sums[g, :, columns] = product
            totals[g, :, columns] = total

    def finish(g):
        for r in range(per_group):
            columns = pl.ds(r * rows, rows)
            place = pl.ds(pl.multiple_of((g * per_group + r) * head, head), head)
            normed = sums[g, :, columns] * (1.0 / totals[g, :, columns])
            stage[:, place] = jnp.transpose(normed).astype(jnp.bfloat16)
        out_copy(g).start()

    lag = middle.astype(jnp.int32)

    def step_body(step, carry):
        left, right = me - step, me + step
        arrives = jnp.logical_and(step > 0, step <= last_step)
        from_left = jnp.logical_and(arrives, left >= 0)
        from_right = jnp.logical_and(arrives, right <= devices - 1)
        span = step - lag
        near, far = me - span, me + span

        @pl.when(from_left)
        def _():
            scale_copy(left, me, scale_right).wait_recv()

            @pl.when(has_right)
            def _():
                scale_copy(left, me + 1, scale_right).start()

        @pl.when(from_right)
        def _():
            scale_copy(right, me, scale_left).wait_recv()

            @pl.when(has_left)
            def _():
                scale_copy(right, me - 1, scale_left).start()

        def chunk_body(g, inner):
            @pl.when(from_left)
            def _():
                code_copy(left, g, me, send_right).wait_recv()

                @pl.when(has_right)
                def _():
                    code_copy(left, g, me + 1, send_right).start()

            @pl.when(from_right)
            def _():
                code_copy(right, g, me, send_left).wait_recv()

                @pl.when(has_left)
                def _():
                    code_copy(right, g, me - 1, send_left).start()

            @pl.when(span == 0)
            def _():
                attend(me, g, first=True)

            @pl.when(jnp.logical_and(span > 0, near >= 0))
            def _():
                attend(near, g)

            @pl.when(jnp.logical_and(span > 0, far <= devices - 1))
            def _():
                attend(far, g)

            @pl.when(span == last_step)
            def _():
                finish(g)

            return inner

        lax.fori_loop(0, kv_heads, chunk_body, 0)
        return carry

    lax.fori_loop(lag, last_step + lag + 1, step_body, 0)

    def drain(tile, carry):
        @pl.when(jnp.logical_and(tile <= me, has_right))
        def _():
            scale_copy(tile, me + 1, scale_right).wait_send()
            pltpu.make_async_copy(codes.at[tile], codes.at[tile], send_right.at[tile]).wait()

        @pl.when(jnp.logical_and(tile >= me, has_left))
        def _():
            scale_copy(tile, me - 1, scale_left).wait_send()
            pltpu.make_async_copy(codes.at[tile], codes.at[tile], send_left.at[tile]).wait()

        return carry

    lax.fori_loop(0, devices, drain, 0)

    def flush(g, carry):
        out_copy(g).wait()
        return carry

    lax.fori_loop(0, kv_heads, flush, 0)


def place_kernel(pieces, from_ref, to_ref, sems):
    rows = from_ref.shape[0] // pieces
    copies = [
        pltpu.make_async_copy(
            from_ref.at[pl.ds(p * rows, rows)], to_ref.at[pl.ds(p * rows, rows)], sems.at[p]
        )
        for p in range(pieces)
    ]
    for copy in copies:
        copy.start()
    for copy in copies:
        copy.wait()


def local(devices, queries, key_codes, value_codes, key_scales, value_scales, masks):
    rows, width = queries.shape
    kv_heads = key_scales.shape[1]
    masks = jnp.transpose(masks, (1, 2, 0))
    heads = masks.shape[2]
    head = width // heads
    per_group = heads // kv_heads
    tall = per_group * rows
    pieces = rows // 16
    hbm = pl.BlockSpec(memory_space=pltpu.HBM)
    dma = pltpu.SemaphoreType.DMA
    scores = heads * rows * rows * devices
    attended = pl.pallas_call(
        functools.partial(attention_kernel, devices, kv_heads, per_group, head, rows),
        out_shape=jax.ShapeDtypeStruct((rows, width), jnp.bfloat16),
        in_specs=[hbm] * 6,
        out_specs=hbm,
        scratch_shapes=[
            pltpu.VMEM((rows, width), jnp.bfloat16),
            pltpu.VMEM((kv_heads, head, tall), jnp.bfloat16),
            pltpu.VMEM((devices, kv_heads, 2 * rows, head), jnp.bfloat16),
            pltpu.VMEM((devices, 2 * kv_heads, head), jnp.bfloat16),
            pltpu.VMEM((kv_heads, 1, tall), jnp.float32),
            pltpu.VMEM((kv_heads, 1, tall), jnp.float32),
            pltpu.VMEM((kv_heads, head, tall), jnp.float32),
            pltpu.VMEM((rows, width), jnp.bfloat16),
            pltpu.VMEM(key_scales.shape, jnp.bfloat16),
            pltpu.VMEM(value_scales.shape, jnp.bfloat16),
            pltpu.SMEM(masks.shape, jnp.int32),
            dma,
            dma((3,)),
            dma((kv_heads, 2)),
            dma((devices,)),
            dma((devices,)),
            dma((devices,)),
            dma((devices,)),
            dma((devices, kv_heads)),
            dma((devices,)),
            dma((kv_heads,)),
        ],
        compiler_params=pltpu.CompilerParams(
            collective_id=0, has_side_effects=True, vmem_limit_bytes=63 * 1024 * 1024
        ),
        cost_estimate=pl.CostEstimate(
            flops=4 * scores * head, bytes_accessed=4 * rows * width, transcendentals=scores
        ),
    )(queries, key_codes, value_codes, key_scales, value_scales, masks)
    return pl.pallas_call(
        functools.partial(place_kernel, pieces),
        out_shape=jax.ShapeDtypeStruct((rows, width), jnp.bfloat16),
        in_specs=[hbm],
        out_specs=hbm,
        scratch_shapes=[dma((pieces,))],
        compiler_params=pltpu.CompilerParams(vmem_limit_bytes=63 * 1024 * 1024),
        cost_estimate=pl.CostEstimate(
            flops=0, bytes_accessed=4 * rows * width, transcendentals=0
        ),
    )(attended)


def solution(mesh):
    both = P(("clip", "sp"), None)
    return jax.shard_map(
        functools.partial(local, mesh.shape["sp"]),
        mesh=mesh,
        in_specs=(both, both, both, both, both, P("clip", None, None)),
        out_specs=both,
        check_vma=False,
    )
```

```python
import functools
import math

import jax
import jax.numpy as jnp
from jax import lax
from jax.experimental import pallas as pl
from jax.experimental.pallas import tpu as pltpu
from jax.sharding import PartitionSpec as P

NEGATIVE = -1e30
MESH = pl.DeviceIdType.MESH


def attention_kernel(
    devices, kv_heads, per_group, head, rows,
    q_hbm, k_hbm, v_hbm, key_scale_hbm, value_scale_hbm, masks_hbm, out_ref,
    q_ref, q_turned, codes, scales, tops, totals, sums,
    key_scale_ref, value_scale_ref, masks_ref,
    q_sem, small_sem, own_sem, send_right, send_left, scale_right, scale_left,
    recv_sem, scale_recv,
):
    me = lax.axis_index("sp")
    has_left = me > 0
    has_right = me < devices - 1
    middle = jnp.logical_and(has_left, has_right)
    last_step = jnp.maximum(me, devices - 1 - me)
    wide = per_group * head
    pair = 2 if per_group % 2 == 0 else 1
    factor = math.log2(math.e) / math.sqrt(head)

    barrier = pltpu.get_barrier_semaphore()

    @pl.when(has_left)
    def _():
        pl.semaphore_signal(barrier, inc=1, device_id={"sp": me - 1}, device_id_type=MESH)

    @pl.when(has_right)
    def _():
        pl.semaphore_signal(barrier, inc=1, device_id={"sp": me + 1}, device_id_type=MESH)

    def own_copies(g):
        columns = pl.ds(pl.multiple_of(g * head, head), head)
        return (
            pltpu.make_async_copy(
                k_hbm.at[:, columns], codes.at[me, g, pl.ds(0, rows)], own_sem.at[g, 0]
            ),
            pltpu.make_async_copy(
                v_hbm.at[:, columns], codes.at[me, g, pl.ds(rows, rows)], own_sem.at[g, 1]
            ),
        )

    def q_copy():
        return pltpu.make_async_copy(q_hbm, q_ref, q_sem)

    def small_copies():
        return (
            pltpu.make_async_copy(key_scale_hbm, key_scale_ref, small_sem.at[0]),
            pltpu.make_async_copy(value_scale_hbm, value_scale_ref, small_sem.at[1]),
            pltpu.make_async_copy(masks_hbm, masks_ref, small_sem.at[2]),
        )

    def code_copy(tile, g, to, send):
        return pltpu.make_async_remote_copy(
            src_ref=codes.at[tile, g],
            dst_ref=codes.at[tile, g],
            send_sem=send.at[tile],
            recv_sem=recv_sem.at[tile, g],
            device_id={"sp": to},
            device_id_type=MESH,
        )

    def scale_copy(tile, to, send):
        return pltpu.make_async_remote_copy(
            src_ref=scales.at[tile],
            dst_ref=scales.at[tile],
            send_sem=send.at[tile],
            recv_sem=scale_recv.at[tile],
            device_id={"sp": to},
            device_id_type=MESH,
        )

    for copy in small_copies():
        copy.start()
    for g in range(kv_heads):
        for copy in own_copies(g):
            copy.start()
    q_copy().start()

    def column(ref):
        spread = jnp.broadcast_to(ref[...].astype(jnp.float32), (kv_heads, kv_heads))
        place = lax.broadcasted_iota(jnp.int32, (kv_heads, kv_heads), 0)
        other = lax.broadcasted_iota(jnp.int32, (kv_heads, kv_heads), 1)
        picked = jnp.sum(jnp.where(place == other, spread, 0.0), axis=1, keepdims=True)
        return jnp.broadcast_to(picked, (kv_heads, head))

    for copy in small_copies():
        copy.wait()
    scales[me] = jnp.concatenate(
        [column(key_scale_ref), column(value_scale_ref)], axis=0
    ).astype(jnp.bfloat16)

    pl.semaphore_wait(barrier, has_left.astype(jnp.int32) + has_right.astype(jnp.int32))

    @pl.when(has_right)
    def _():
        scale_copy(me, me + 1, scale_right).start()

    @pl.when(has_left)
    def _():
        scale_copy(me, me - 1, scale_left).start()

    def send_own(g, carry):
        for copy in own_copies(g):
            copy.wait()

        @pl.when(has_right)
        def _():
            code_copy(me, g, me + 1, send_right).start()

        @pl.when(has_left)
        def _():
            code_copy(me, g, me - 1, send_left).start()

        return carry

    lax.fori_loop(0, kv_heads, send_own, 0)
    q_copy().wait()

    ones = jnp.ones((16, rows), jnp.bfloat16)

    def put(g, r, normed):
        for o in range(pair):
            place = pl.ds(pl.multiple_of((g * per_group + r + o) * head, head), head)
            piece = normed[:, o * rows : (o + 1) * rows]
            out_ref[:, place] = jnp.transpose(piece).astype(jnp.bfloat16)

    def attend(tile, g, first=False, last=False):
        both = scales[tile].astype(jnp.float32)
        place = lax.broadcasted_iota(jnp.int32, both.shape, 0)
        key_scale = jnp.sum(jnp.where(place == g, both, 0.0), axis=0, keepdims=True)
        value_scale = jnp.sum(jnp.where(place == g + kv_heads, both, 0.0), axis=0, keepdims=True)
        key_scale = jnp.concatenate([key_scale * factor] * pair, axis=1)
        value_scale = jnp.concatenate([value_scale] * pair, axis=1)
        keys = codes[tile, g, :rows, :]
        values = jnp.concatenate([jnp.transpose(codes[tile, g, rows:, :]), ones], axis=0)
        for r in range(0, per_group, pair):
            columns = pl.ds(r * rows, pair * rows)
            if first:
                queries = jnp.concatenate(
                    [
                        jnp.transpose(
                            q_ref[:, pl.ds(pl.multiple_of((g * per_group + o) * head, head), head)]
                        )
                        for o in range(r, r + pair)
                    ],
                    axis=1,
                )
                q_turned[g, :, columns] = queries
            else:
                queries = q_turned[g, :, columns]
            raw = jnp.dot(keys, queries, preferred_element_type=jnp.float32)
            bias = jnp.concatenate(
                [
                    jnp.full(
                        (1, rows),
                        jnp.where(masks_ref[me, tile, g * per_group + o] > 0, 0.0, NEGATIVE),
                        jnp.float32,
                    )
                    for o in range(r, r + pair)
                ],
                axis=1,
            )
            top = jnp.max(raw, axis=0, keepdims=True) * key_scale + bias
            if not first:
                before = tops[g, :, columns]
                top = jnp.maximum(before, top)
                rescale = jnp.exp2(before - top)
            if not last:
                tops[g, :, columns] = top
            expo = jnp.exp2(raw * key_scale - (top - bias)).astype(jnp.bfloat16)
            added = jnp.dot(values, expo, preferred_element_type=jnp.float32)
            product = added[:head] * value_scale
            total = added[head : head + 1]
            if not first:
                product = product + sums[g, :, columns] * rescale
                total = total + totals[g, :, columns] * rescale
            if last:
                put(g, r, product * (1.0 / total))
            else:
                sums[g, :, columns] = product
                totals[g, :, columns] = total

    def finish(g):
        for r in range(0, per_group, pair):
            columns = pl.ds(r * rows, pair * rows)
            put(g, r, sums[g, :, columns] * (1.0 / totals[g, :, columns]))

    lag = middle.astype(jnp.int32)

    def step_body(step, carry):
        left, right = me - step, me + step
        arrives = jnp.logical_and(step > 0, step <= last_step)
        from_left = jnp.logical_and(arrives, left >= 0)
        from_right = jnp.logical_and(arrives, right <= devices - 1)
        span = step - lag
        near, far = me - span, me + span
        between = span > 0
        if devices % 2 == 0:
            between = jnp.logical_and(between, span < last_step)

        @pl.when(from_left)
        def _():
            scale_copy(left, me, scale_right).wait_recv()

            @pl.when(has_right)
            def _():
                scale_copy(left, me + 1, scale_right).start()

        @pl.when(from_right)
        def _():
            scale_copy(right, me, scale_left).wait_recv()

            @pl.when(has_left)
            def _():
                scale_copy(right, me - 1, scale_left).start()

        def chunk_body(g, inner):
            @pl.when(from_left)
            def _():
                code_copy(left, g, me, send_right).wait_recv()

                @pl.when(has_right)
                def _():
                    code_copy(left, g, me + 1, send_right).start()

            @pl.when(from_right)
            def _():
                code_copy(right, g, me, send_left).wait_recv()

                @pl.when(has_left)
                def _():
                    code_copy(right, g, me - 1, send_left).start()

            @pl.when(span == 0)
            def _():
                attend(me, g, first=True)

            @pl.when(jnp.logical_and(between, near >= 0))
            def _():
                attend(near, g)

            @pl.when(jnp.logical_and(between, far <= devices - 1))
            def _():
                attend(far, g)

            @pl.when(span == last_step)
            def _():
                if devices % 2 == 0:
                    attend(jnp.where(near >= 0, near, far), g, last=True)
                else:
                    finish(g)

            return inner

        lax.fori_loop(0, kv_heads, chunk_body, 0)
        return carry

    lax.fori_loop(lag, last_step + lag + 1, step_body, 0)

    def drain(tile, carry):
        @pl.when(jnp.logical_and(tile <= me, has_right))
        def _():
            scale_copy(tile, me + 1, scale_right).wait_send()
            pltpu.make_async_copy(codes.at[tile], codes.at[tile], send_right.at[tile]).wait()

        @pl.when(jnp.logical_and(tile >= me, has_left))
        def _():
            scale_copy(tile, me - 1, scale_left).wait_send()
            pltpu.make_async_copy(codes.at[tile], codes.at[tile], send_left.at[tile]).wait()

        return carry

    lax.fori_loop(0, devices, drain, 0)


def local(devices, queries, key_codes, value_codes, key_scales, value_scales, masks):
    rows, width = queries.shape
    kv_heads = key_scales.shape[1]
    masks = jnp.transpose(masks, (1, 2, 0))
    heads = masks.shape[2]
    head = width // heads
    per_group = heads // kv_heads
    tall = per_group * rows
    hbm = pl.BlockSpec(memory_space=pltpu.HBM)
    dma = pltpu.SemaphoreType.DMA
    scores = heads * rows * rows * devices
    return pl.pallas_call(
        functools.partial(attention_kernel, devices, kv_heads, per_group, head, rows),
        out_shape=jax.ShapeDtypeStruct((rows, width), jnp.bfloat16),
        in_specs=[hbm] * 6,
        out_specs=pl.BlockSpec(memory_space=pltpu.VMEM),
        scratch_shapes=[
            pltpu.VMEM((rows, width), jnp.bfloat16),
            pltpu.VMEM((kv_heads, head, tall), jnp.bfloat16),
            pltpu.VMEM((devices, kv_heads, 2 * rows, head), jnp.bfloat16),
            pltpu.VMEM((devices, 2 * kv_heads, head), jnp.bfloat16),
            pltpu.VMEM((kv_heads, 1, tall), jnp.float32),
            pltpu.VMEM((kv_heads, 1, tall), jnp.float32),
            pltpu.VMEM((kv_heads, head, tall), jnp.float32),
            pltpu.VMEM(key_scales.shape, jnp.bfloat16),
            pltpu.VMEM(value_scales.shape, jnp.bfloat16),
            pltpu.SMEM(masks.shape, jnp.int32),
            dma,
            dma((3,)),
            dma((kv_heads, 2)),
            dma((devices,)),
            dma((devices,)),
            dma((devices,)),
            dma((devices,)),
            dma((devices, kv_heads)),
            dma((devices,)),
        ],
        compiler_params=pltpu.CompilerParams(
            collective_id=0, has_side_effects=True, vmem_limit_bytes=40 * 1024 * 1024
        ),
        cost_estimate=pl.CostEstimate(
            flops=4 * scores * head, bytes_accessed=4 * rows * width, transcendentals=scores
        ),
    )(
        *(
            pltpu.with_memory_space_constraint(operand, pltpu.HBM)
            for operand in (queries, key_codes, value_codes, key_scales, value_scales, masks)
        )
    )


def solution(mesh):
    both = P(("clip", "sp"), None)
    return jax.shard_map(
        functools.partial(local, mesh.shape["sp"]),
        mesh=mesh,
        in_specs=(both, both, both, both, both, P("clip", None, None)),
        out_specs=both,
        check_vma=False,
    )
```

```python
import functools
import math

import jax
import jax.numpy as jnp
from jax import lax
from jax.experimental import pallas as pl
from jax.experimental.pallas import tpu as pltpu
from jax.sharding import PartitionSpec as P

NEGATIVE = -1e30
MESH = pl.DeviceIdType.MESH


def attention_kernel(
    devices, kv_heads, per_group, head, rows,
    q_hbm, k_hbm, v_hbm, key_scale_hbm, value_scale_hbm, masks_hbm, out_ref,
    q_ref, q_turned, codes, scales, tops, totals, sums,
    key_scale_ref, value_scale_ref, masks_ref,
    q_sem, small_sem, own_sem, send_right, send_left, scale_right, scale_left,
    recv_sem, scale_recv, ready,
):
    me = lax.axis_index("sp")
    has_left = me > 0
    has_right = me < devices - 1
    middle = jnp.logical_and(has_left, has_right)
    last_step = jnp.maximum(me, devices - 1 - me)
    wide = per_group * head
    pair = 2 if per_group % 2 == 0 else 1
    factor = math.log2(math.e) / math.sqrt(head)

    barrier = pltpu.get_barrier_semaphore()

    @pl.when(has_right)
    def _():
        pl.semaphore_signal(barrier, inc=1, device_id={"sp": me + 1}, device_id_type=MESH)

    def own_copies(g):
        columns = pl.ds(pl.multiple_of(g * head, head), head)
        return (
            pltpu.make_async_copy(
                k_hbm.at[:, columns], codes.at[me, g, pl.ds(0, rows)], own_sem.at[g, 0]
            ),
            pltpu.make_async_copy(
                v_hbm.at[:, columns], codes.at[me, g, pl.ds(rows, rows)], own_sem.at[g, 1]
            ),
        )

    def q_copy():
        return pltpu.make_async_copy(q_hbm, q_ref, q_sem)

    def small_copies():
        return (
            pltpu.make_async_copy(key_scale_hbm, key_scale_ref, small_sem.at[0]),
            pltpu.make_async_copy(value_scale_hbm, value_scale_ref, small_sem.at[1]),
            pltpu.make_async_copy(masks_hbm, masks_ref, small_sem.at[2]),
        )

    def code_copy(tile, g, to, send):
        return pltpu.make_async_remote_copy(
            src_ref=codes.at[tile, g],
            dst_ref=codes.at[tile, g],
            send_sem=send.at[tile],
            recv_sem=recv_sem.at[tile, g],
            device_id={"sp": to},
            device_id_type=MESH,
        )

    def scale_copy(tile, to, send):
        return pltpu.make_async_remote_copy(
            src_ref=scales.at[tile],
            dst_ref=scales.at[tile],
            send_sem=send.at[tile],
            recv_sem=scale_recv.at[tile],
            device_id={"sp": to},
            device_id_type=MESH,
        )

    for copy in small_copies():
        copy.start()
    for g in range(kv_heads):
        for copy in own_copies(g):
            copy.start()
    q_copy().start()

    def column(ref):
        spread = jnp.broadcast_to(ref[...].astype(jnp.float32), (kv_heads, kv_heads))
        place = lax.broadcasted_iota(jnp.int32, (kv_heads, kv_heads), 0)
        other = lax.broadcasted_iota(jnp.int32, (kv_heads, kv_heads), 1)
        picked = jnp.sum(jnp.where(place == other, spread, 0.0), axis=1, keepdims=True)
        return jnp.broadcast_to(picked, (kv_heads, head))

    @pl.when(has_left)
    def _():
        pl.semaphore_wait(barrier, 1)
        pl.semaphore_signal(ready, inc=1, device_id={"sp": me - 1}, device_id_type=MESH)

    for copy in small_copies():
        copy.wait()
    scales[me] = jnp.concatenate(
        [column(key_scale_ref), column(value_scale_ref)], axis=0
    ).astype(jnp.bfloat16)

    @pl.when(has_left)
    def _():
        scale_copy(me, me - 1, scale_left).start()

    def send_left_own(g, carry):
        for copy in own_copies(g):
            copy.wait()

        @pl.when(has_left)
        def _():
            code_copy(me, g, me - 1, send_left).start()

        return carry

    lax.fori_loop(0, kv_heads, send_left_own, 0)

    @pl.when(has_right)
    def _():
        pl.semaphore_wait(ready, 1)
        scale_copy(me, me + 1, scale_right).start()

        def send_right_own(g, carry):
            code_copy(me, g, me + 1, send_right).start()
            return carry

        lax.fori_loop(0, kv_heads, send_right_own, 0)

    q_copy().wait()

    ones = jnp.ones((16, rows), jnp.bfloat16)

    def put(g, r, normed):
        for o in range(pair):
            place = pl.ds(pl.multiple_of((g * per_group + r + o) * head, head), head)
            piece = normed[:, o * rows : (o + 1) * rows]
            out_ref[:, place] = jnp.transpose(piece).astype(jnp.bfloat16)

    def attend(tile, g, first=False, last=False):
        both = scales[tile].astype(jnp.float32)
        place = lax.broadcasted_iota(jnp.int32, both.shape, 0)
        key_scale = jnp.sum(jnp.where(place == g, both, 0.0), axis=0, keepdims=True)
        value_scale = jnp.sum(jnp.where(place == g + kv_heads, both, 0.0), axis=0, keepdims=True)
        key_scale = jnp.concatenate([key_scale * factor] * pair, axis=1)
        value_scale = jnp.concatenate([value_scale] * pair, axis=1)
        keys = codes[tile, g, :rows, :]
        values = jnp.concatenate([jnp.transpose(codes[tile, g, rows:, :]), ones], axis=0)
        for r in range(0, per_group, pair):
            columns = pl.ds(r * rows, pair * rows)
            if first:
                queries = jnp.concatenate(
                    [
                        jnp.transpose(
                            q_ref[:, pl.ds(pl.multiple_of((g * per_group + o) * head, head), head)]
                        )
                        for o in range(r, r + pair)
                    ],
                    axis=1,
                )
                q_turned[g, :, columns] = queries
            else:
                queries = q_turned[g, :, columns]
            raw = jnp.dot(keys, queries, preferred_element_type=jnp.float32)
            bias = jnp.concatenate(
                [
                    jnp.full(
                        (1, rows),
                        jnp.where(masks_ref[me, tile, g * per_group + o] > 0, 0.0, NEGATIVE),
                        jnp.float32,
                    )
                    for o in range(r, r + pair)
                ],
                axis=1,
            )
            top = jnp.max(raw, axis=0, keepdims=True) * key_scale + bias
            if not first:
                before = tops[g, :, columns]
                top = jnp.maximum(before, top)
                rescale = jnp.exp2(before - top)
            if not last:
                tops[g, :, columns] = top
            expo = jnp.exp2(raw * key_scale - (top - bias)).astype(jnp.bfloat16)
            added = jnp.dot(values, expo, preferred_element_type=jnp.float32)
            product = added[:head] * value_scale
            total = added[head : head + 1]
            if not first:
                product = product + sums[g, :, columns] * rescale
                total = total + totals[g, :, columns] * rescale
            if last:
                put(g, r, product * (1.0 / total))
            else:
                sums[g, :, columns] = product
                totals[g, :, columns] = total

    def finish(g):
        for r in range(0, per_group, pair):
            columns = pl.ds(r * rows, pair * rows)
            put(g, r, sums[g, :, columns] * (1.0 / totals[g, :, columns]))

    lag = middle.astype(jnp.int32)

    def step_body(step, carry):
        left, right = me - step, me + step
        arrives = jnp.logical_and(step > 0, step <= last_step)
        from_left = jnp.logical_and(arrives, left >= 0)
        from_right = jnp.logical_and(arrives, right <= devices - 1)
        span = step - lag
        near, far = me - span, me + span
        between = span > 0
        if devices % 2 == 0:
            between = jnp.logical_and(between, span < last_step)

        @pl.when(from_left)
        def _():
            scale_copy(left, me, scale_right).wait_recv()

            @pl.when(has_right)
            def _():
                scale_copy(left, me + 1, scale_right).start()

        @pl.when(from_right)
        def _():
            scale_copy(right, me, scale_left).wait_recv()

            @pl.when(has_left)
            def _():
                scale_copy(right, me - 1, scale_left).start()

        def chunk_body(g, inner):
            @pl.when(from_left)
            def _():
                code_copy(left, g, me, send_right).wait_recv()

                @pl.when(has_right)
                def _():
                    code_copy(left, g, me + 1, send_right).start()

            @pl.when(from_right)
            def _():
                code_copy(right, g, me, send_left).wait_recv()

                @pl.when(has_left)
                def _():
                    code_copy(right, g, me - 1, send_left).start()

            @pl.when(span == 0)
            def _():
                attend(me, g, first=True)

            @pl.when(jnp.logical_and(between, near >= 0))
            def _():
                attend(near, g)

            @pl.when(jnp.logical_and(between, far <= devices - 1))
            def _():
                attend(far, g)

            @pl.when(span == last_step)
            def _():
                if devices % 2 == 0:
                    attend(jnp.where(near >= 0, near, far), g, last=True)
                else:
                    finish(g)

            return inner

        lax.fori_loop(0, kv_heads, chunk_body, 0)
        return carry

    lax.fori_loop(lag, last_step + lag + 1, step_body, 0)

    def drain(tile, carry):
        @pl.when(jnp.logical_and(tile <= me, has_right))
        def _():
            scale_copy(tile, me + 1, scale_right).wait_send()
            pltpu.make_async_copy(codes.at[tile], codes.at[tile], send_right.at[tile]).wait()

        @pl.when(jnp.logical_and(tile >= me, has_left))
        def _():
            scale_copy(tile, me - 1, scale_left).wait_send()
            pltpu.make_async_copy(codes.at[tile], codes.at[tile], send_left.at[tile]).wait()

        return carry

    lax.fori_loop(0, devices, drain, 0)


def local(devices, queries, key_codes, value_codes, key_scales, value_scales, masks):
    rows, width = queries.shape
    kv_heads = key_scales.shape[1]
    masks = jnp.transpose(masks, (1, 2, 0))
    heads = masks.shape[2]
    head = width // heads
    per_group = heads // kv_heads
    tall = per_group * rows
    hbm = pl.BlockSpec(memory_space=pltpu.HBM)
    dma = pltpu.SemaphoreType.DMA
    scores = heads * rows * rows * devices
    return pl.pallas_call(
        functools.partial(attention_kernel, devices, kv_heads, per_group, head, rows),
        out_shape=jax.ShapeDtypeStruct((rows, width), jnp.bfloat16),
        in_specs=[hbm] * 6,
        out_specs=pl.BlockSpec(memory_space=pltpu.VMEM),
        scratch_shapes=[
            pltpu.VMEM((rows, width), jnp.bfloat16),
            pltpu.VMEM((kv_heads, head, tall), jnp.bfloat16),
            pltpu.VMEM((devices, kv_heads, 2 * rows, head), jnp.bfloat16),
            pltpu.VMEM((devices, 2 * kv_heads, head), jnp.bfloat16),
            pltpu.VMEM((kv_heads, 1, tall), jnp.float32),
            pltpu.VMEM((kv_heads, 1, tall), jnp.float32),
            pltpu.VMEM((kv_heads, head, tall), jnp.float32),
            pltpu.VMEM(key_scales.shape, jnp.bfloat16),
            pltpu.VMEM(value_scales.shape, jnp.bfloat16),
            pltpu.SMEM(masks.shape, jnp.int32),
            dma,
            dma((3,)),
            dma((kv_heads, 2)),
            dma((devices,)),
            dma((devices,)),
            dma((devices,)),
            dma((devices,)),
            dma((devices, kv_heads)),
            dma((devices,)),
            pltpu.SemaphoreType.REGULAR,
        ],
        compiler_params=pltpu.CompilerParams(
            collective_id=0, has_side_effects=True, vmem_limit_bytes=40 * 1024 * 1024
        ),
        cost_estimate=pl.CostEstimate(
            flops=4 * scores * head, bytes_accessed=4 * rows * width, transcendentals=scores
        ),
    )(
        *(
            pltpu.with_memory_space_constraint(operand, pltpu.HBM)
            for operand in (queries, key_codes, value_codes, key_scales, value_scales, masks)
        )
    )


def solution(mesh):
    both = P(("clip", "sp"), None)
    return jax.shard_map(
        functools.partial(local, mesh.shape["sp"]),
        mesh=mesh,
        in_specs=(both, both, both, both, both, P("clip", None, None)),
        out_specs=both,
        check_vma=False,
    )
```

```python
import functools
import math

import jax
import jax.numpy as jnp
from jax import lax
from jax.experimental import pallas as pl
from jax.experimental.pallas import tpu as pltpu
from jax.sharding import PartitionSpec as P

NEGATIVE = -1e30
MESH = pl.DeviceIdType.MESH


def attention_kernel(
    devices, kv_heads, per_group, head, rows,
    q_hbm, k_hbm, v_hbm, key_scale_hbm, value_scale_hbm, masks_hbm, out_ref,
    q_ref, q_turned, codes, scales, tops, totals, sums,
    key_scale_ref, value_scale_ref, masks_ref,
    q_sem, small_sem, own_sem, send_right, send_left, scale_right, scale_left,
    recv_sem, scale_recv, ready,
):
    me = lax.axis_index("sp")
    has_left = me > 0
    has_right = me < devices - 1
    middle = jnp.logical_and(has_left, has_right)
    last_step = jnp.maximum(me, devices - 1 - me)
    wide = per_group * head
    pair = 2 if per_group % 2 == 0 else 1
    factor = math.log2(math.e) / math.sqrt(head)

    barrier = pltpu.get_barrier_semaphore()

    @pl.when(has_right)
    def _():
        pl.semaphore_signal(barrier, inc=1, device_id={"sp": me + 1}, device_id_type=MESH)

    def own_copies(g):
        columns = pl.ds(pl.multiple_of(g * head, head), head)
        return (
            pltpu.make_async_copy(
                k_hbm.at[:, columns], codes.at[me, g, pl.ds(0, rows)], own_sem.at[g, 0]
            ),
            pltpu.make_async_copy(
                v_hbm.at[:, columns], codes.at[me, g, pl.ds(rows, rows)], own_sem.at[g, 1]
            ),
        )

    def q_copy():
        return pltpu.make_async_copy(q_hbm, q_ref, q_sem)

    def small_copies():
        return (
            pltpu.make_async_copy(key_scale_hbm, key_scale_ref, small_sem.at[0]),
            pltpu.make_async_copy(value_scale_hbm, value_scale_ref, small_sem.at[1]),
            pltpu.make_async_copy(masks_hbm, masks_ref, small_sem.at[2]),
        )

    def code_copy(tile, g, to, send):
        return pltpu.make_async_remote_copy(
            src_ref=codes.at[tile, g],
            dst_ref=codes.at[tile, g],
            send_sem=send.at[tile],
            recv_sem=recv_sem.at[tile, g],
            device_id={"sp": to},
            device_id_type=MESH,
        )

    def scale_copy(tile, to, send):
        return pltpu.make_async_remote_copy(
            src_ref=scales.at[tile],
            dst_ref=scales.at[tile],
            send_sem=send.at[tile],
            recv_sem=scale_recv.at[tile],
            device_id={"sp": to},
            device_id_type=MESH,
        )

    for copy in small_copies():
        copy.start()
    for g in range(kv_heads):
        for copy in own_copies(g):
            copy.start()
    q_copy().start()

    def column(ref):
        spread = jnp.broadcast_to(ref[...].astype(jnp.float32), (kv_heads, kv_heads))
        place = lax.broadcasted_iota(jnp.int32, (kv_heads, kv_heads), 0)
        other = lax.broadcasted_iota(jnp.int32, (kv_heads, kv_heads), 1)
        picked = jnp.sum(jnp.where(place == other, spread, 0.0), axis=1, keepdims=True)
        return jnp.broadcast_to(picked, (kv_heads, head))

    @pl.when(has_left)
    def _():
        pl.semaphore_wait(barrier, 1)
        pl.semaphore_signal(ready, inc=1, device_id={"sp": me - 1}, device_id_type=MESH)

    def send_left_own(g, carry):
        for copy in own_copies(g):
            copy.wait()

        @pl.when(has_left)
        def _():
            code_copy(me, g, me - 1, send_left).start()

        return carry

    lax.fori_loop(0, 1, send_left_own, 0)

    for copy in small_copies():
        copy.wait()
    scales[me] = jnp.concatenate(
        [column(key_scale_ref), column(value_scale_ref)], axis=0
    ).astype(jnp.bfloat16)

    @pl.when(has_left)
    def _():
        scale_copy(me, me - 1, scale_left).start()

    lax.fori_loop(1, kv_heads, send_left_own, 0)

    @pl.when(has_right)
    def _():
        pl.semaphore_wait(ready, 1)
        scale_copy(me, me + 1, scale_right).start()

        def send_right_own(g, carry):
            code_copy(me, g, me + 1, send_right).start()
            return carry

        lax.fori_loop(0, kv_heads, send_right_own, 0)

    q_copy().wait()

    ones = jnp.ones((16, rows), jnp.bfloat16)

    def put(g, r, normed):
        for o in range(pair):
            place = pl.ds(pl.multiple_of((g * per_group + r + o) * head, head), head)
            piece = normed[:, o * rows : (o + 1) * rows]
            out_ref[:, place] = jnp.transpose(piece).astype(jnp.bfloat16)

    def attend(tile, g, first=False, last=False):
        both = scales[tile].astype(jnp.float32)
        place = lax.broadcasted_iota(jnp.int32, both.shape, 0)
        key_scale = jnp.sum(jnp.where(place == g, both, 0.0), axis=0, keepdims=True)
        value_scale = jnp.sum(jnp.where(place == g + kv_heads, both, 0.0), axis=0, keepdims=True)
        key_scale = jnp.concatenate([key_scale * factor] * pair, axis=1)
        value_scale = jnp.concatenate([value_scale] * pair, axis=1)
        keys = codes[tile, g, :rows, :]
        values = jnp.concatenate([jnp.transpose(codes[tile, g, rows:, :]), ones], axis=0)
        for r in range(0, per_group, pair):
            columns = pl.ds(r * rows, pair * rows)
            if first:
                queries = jnp.concatenate(
                    [
                        jnp.transpose(
                            q_ref[:, pl.ds(pl.multiple_of((g * per_group + o) * head, head), head)]
                        )
                        for o in range(r, r + pair)
                    ],
                    axis=1,
                )
                q_turned[g, :, columns] = queries
            else:
                queries = q_turned[g, :, columns]
            raw = jnp.dot(keys, queries, preferred_element_type=jnp.float32)
            bias = jnp.concatenate(
                [
                    jnp.full(
                        (1, rows),
                        jnp.where(masks_ref[me, tile, g * per_group + o] > 0, 0.0, NEGATIVE),
                        jnp.float32,
                    )
                    for o in range(r, r + pair)
                ],
                axis=1,
            )
            top = jnp.max(raw, axis=0, keepdims=True) * key_scale + bias
            if not first:
                before = tops[g, :, columns]
                top = jnp.maximum(before, top)
                rescale = jnp.exp2(before - top)
            if not last:
                tops[g, :, columns] = top
            expo = jnp.exp2(raw * key_scale - (top - bias)).astype(jnp.bfloat16)
            added = jnp.dot(values, expo, preferred_element_type=jnp.float32)
            product = added[:head] * value_scale
            total = added[head : head + 1]
            if not first:
                product = product + sums[g, :, columns] * rescale
                total = total + totals[g, :, columns] * rescale
            if last:
                put(g, r, product * (1.0 / total))
            else:
                sums[g, :, columns] = product
                totals[g, :, columns] = total

    def finish(g):
        for r in range(0, per_group, pair):
            columns = pl.ds(r * rows, pair * rows)
            put(g, r, sums[g, :, columns] * (1.0 / totals[g, :, columns]))

    lag = middle.astype(jnp.int32)

    def step_body(step, carry):
        left, right = me - step, me + step
        arrives = jnp.logical_and(step > 0, step <= last_step)
        from_left = jnp.logical_and(arrives, left >= 0)
        from_right = jnp.logical_and(arrives, right <= devices - 1)
        span = step - lag
        near, far = me - span, me + span
        between = span > 0
        if devices % 2 == 0:
            between = jnp.logical_and(between, span < last_step)

        @pl.when(from_left)
        def _():
            scale_copy(left, me, scale_right).wait_recv()

            @pl.when(has_right)
            def _():
                scale_copy(left, me + 1, scale_right).start()

        @pl.when(from_right)
        def _():
            scale_copy(right, me, scale_left).wait_recv()

            @pl.when(has_left)
            def _():
                scale_copy(right, me - 1, scale_left).start()

        def chunk_body(g, inner):
            @pl.when(from_left)
            def _():
                code_copy(left, g, me, send_right).wait_recv()

                @pl.when(has_right)
                def _():
                    code_copy(left, g, me + 1, send_right).start()

            @pl.when(from_right)
            def _():
                code_copy(right, g, me, send_left).wait_recv()

                @pl.when(has_left)
                def _():
                    code_copy(right, g, me - 1, send_left).start()

            @pl.when(span == 0)
            def _():
                attend(me, g, first=True)

            @pl.when(jnp.logical_and(between, near >= 0))
            def _():
                attend(near, g)

            @pl.when(jnp.logical_and(between, far <= devices - 1))
            def _():
                attend(far, g)

            @pl.when(span == last_step)
            def _():
                if devices % 2 == 0:
                    attend(jnp.where(near >= 0, near, far), g, last=True)
                else:
                    finish(g)

            return inner

        lax.fori_loop(0, kv_heads, chunk_body, 0)
        return carry

    lax.fori_loop(lag, last_step + lag + 1, step_body, 0)

    def drain(tile, carry):
        @pl.when(jnp.logical_and(tile <= me, has_right))
        def _():
            scale_copy(tile, me + 1, scale_right).wait_send()
            pltpu.make_async_copy(codes.at[tile], codes.at[tile], send_right.at[tile]).wait()

        @pl.when(jnp.logical_and(tile >= me, has_left))
        def _():
            scale_copy(tile, me - 1, scale_left).wait_send()
            pltpu.make_async_copy(codes.at[tile], codes.at[tile], send_left.at[tile]).wait()

        return carry

    lax.fori_loop(0, devices, drain, 0)


def local(devices, queries, key_codes, value_codes, key_scales, value_scales, masks):
    rows, width = queries.shape
    kv_heads = key_scales.shape[1]
    masks = jnp.transpose(masks, (1, 2, 0))
    heads = masks.shape[2]
    head = width // heads
    per_group = heads // kv_heads
    tall = per_group * rows
    hbm = pl.BlockSpec(memory_space=pltpu.HBM)
    dma = pltpu.SemaphoreType.DMA
    scores = heads * rows * rows * devices
    return pl.pallas_call(
        functools.partial(attention_kernel, devices, kv_heads, per_group, head, rows),
        out_shape=jax.ShapeDtypeStruct((rows, width), jnp.bfloat16),
        in_specs=[hbm] * 6,
        out_specs=pl.BlockSpec(memory_space=pltpu.VMEM),
        scratch_shapes=[
            pltpu.VMEM((rows, width), jnp.bfloat16),
            pltpu.VMEM((kv_heads, head, tall), jnp.bfloat16),
            pltpu.VMEM((devices, kv_heads, 2 * rows, head), jnp.bfloat16),
            pltpu.VMEM((devices, 2 * kv_heads, head), jnp.bfloat16),
            pltpu.VMEM((kv_heads, 1, tall), jnp.float32),
            pltpu.VMEM((kv_heads, 1, tall), jnp.float32),
            pltpu.VMEM((kv_heads, head, tall), jnp.float32),
            pltpu.VMEM(key_scales.shape, jnp.bfloat16),
            pltpu.VMEM(value_scales.shape, jnp.bfloat16),
            pltpu.SMEM(masks.shape, jnp.int32),
            dma,
            dma((3,)),
            dma((kv_heads, 2)),
            dma((devices,)),
            dma((devices,)),
            dma((devices,)),
            dma((devices,)),
            dma((devices, kv_heads)),
            dma((devices,)),
            pltpu.SemaphoreType.REGULAR,
        ],
        compiler_params=pltpu.CompilerParams(
            collective_id=0, has_side_effects=True, vmem_limit_bytes=40 * 1024 * 1024
        ),
        cost_estimate=pl.CostEstimate(
            flops=4 * scores * head, bytes_accessed=4 * rows * width, transcendentals=scores
        ),
    )(
        *(
            pltpu.with_memory_space_constraint(operand, pltpu.HBM)
            for operand in (queries, key_codes, value_codes, key_scales, value_scales, masks)
        )
    )


def solution(mesh):
    both = P(("clip", "sp"), None)
    return jax.shard_map(
        functools.partial(local, mesh.shape["sp"]),
        mesh=mesh,
        in_specs=(both, both, both, both, both, P("clip", None, None)),
        out_specs=both,
        check_vma=False,
    )
```
